1024 devices in a mesh: dp: 16 (over y, core), table: 64 (over x, z).
Axes of the slice: x: 4, y: 8, z: 16, core: 2. Of those that a mesh axis runs over, the one named last changes fastest.
Arguments:
- queries: bfloat16 [524288, 256], P(('dp', 'table')), may hold values from -6 to 6
- item_rows: bfloat16 [262144, 256], P(('dp', 'table')), may hold values from -1.5 to 1.5
- item_bin: int32 [262144], P(('dp', 'table')), may hold values from 0 to 127
- counts: int32 [1024], P(('dp', 'table')), may hold values from 128 to 256, as said below
- labels: int32 [524288], P(('dp', 'table')), may hold values from 0 to 255, as said below
- owner: int32 [262144], P(('dp', 'table')), may hold values from 0 to 1023, as said below
- local_row: int32 [262144], P(('dp', 'table')), may hold values from 0 to 2047
- logq: float32 [128], replicated, may hold values from -6 to 0
- tower_weight: bfloat16 [256, 256], replicated, may hold values from -0.375 to 0.375
- tower_gain: float32 [256], replicated, may hold values from 0.25 to 1.75
Outputs:
- grad_query: bfloat16 [524288, 256], P(('dp', 'table'))
- grad_table: float32 [2097152, 256], P(('dp', 'table'))
- grad_weight: float32 [256, 256], replicated
- grad_gain: float32 [256], replicated
The draws below stay inside these ranges and needn't reach their ends.
Inputs may be any that keep to these rules, and one draw needn't show every extreme that they name: `counts`: each device's count of live slots; some device has all 256 live. `labels`: a query's positive is a live slot of its own device. owner = dp index * 64 + table index of the owning device. Among the 256 slots of one device at most 32 name owners of one dp index, reached on every device. Take the slots of all devices of one table index t whose owners have dp index a, each device's in slot order, device after device in dp order, the j-th of device b at position b * 32 + j: at most 8 of them name one table index, and this is reached.
All inputs are finite; a program needn't handle non-finite values.
Results may differ from the reference program's by a relative error of at most 0.012.
Values may be sent and summed in bfloat16 or wider, within the bound.
A program may use at most 64 MiB of HBM per device.

```python
import jax
import jax.numpy as jnp
from jax import lax

D = 256
Q_DEV = 512
U_DEV = 256
ROWS_DEV = 2048
BINS = 128
CAP_DP = 32
CAP_T = 8
QUERIES = 524288
ALL_UNIQUE = 262144
TABLE_ROWS = 2097152
N_DP = 16
N_TABLE = 64


def shared_counts(key):
    devices = N_DP * N_TABLE
    drawn = jax.random.randint(jax.random.fold_in(key, 21), (devices,), U_DEV // 2, U_DEV + 1)
    return drawn.at[0].set(U_DEV).astype(jnp.int32)


def draw_counts(key, part):
    return shared_counts(key)


def draw_labels(key, part):
    cnt = shared_counts(key)
    key = jax.random.fold_in(key, 3)
    spread = jnp.repeat(cnt, Q_DEV, total_repeat_length=QUERIES)
    fraction = jax.random.randint(key, (QUERIES,), 0, 65536)
    return (fraction * spread // 65536).astype(jnp.int32)


def draw_owner(key, part):
    key = jax.random.fold_in(key, 11)
    devices = N_DP * N_TABLE
    slot_keys = jax.random.split(jax.random.fold_in(key, 1), devices)
    shuffled = jax.vmap(lambda one: jax.random.permutation(one, U_DEV))(slot_keys).astype(jnp.int32)
    hot_dp = jax.random.randint(jax.random.fold_in(key, 2), (devices, 1), 0, N_DP).astype(jnp.int32)
    spread_dp = jnp.maximum(shuffled - CAP_DP, 0) % (N_DP - 1)
    other_dp = spread_dp + (spread_dp >= hot_dp).astype(jnp.int32)
    dp_of = jnp.where(shuffled < CAP_DP, hot_dp, other_dp).astype(jnp.int32)
    hits = (dp_of[:, :, None] == jnp.arange(N_DP, dtype=jnp.int32)[None, None, :]).astype(jnp.int32)
    place = jnp.sum((jnp.cumsum(hits, axis=1) - hits) * hits, axis=2).astype(jnp.int32)
    load = jnp.sum(hits, axis=1).reshape(N_DP, N_TABLE, N_DP)
    load_grid = jnp.transpose(load, (2, 1, 0))
    span = N_DP * CAP_DP
    position = jnp.arange(span, dtype=jnp.int32)
    occupied = (position % CAP_DP)[None, None, :] < load_grid[:, :, position // CAP_DP]
    grid_keys = jax.random.split(jax.random.fold_in(key, 3), N_DP * N_TABLE)
    mixing = jax.vmap(lambda one: jax.random.permutation(one, span))(grid_keys).astype(jnp.int32).reshape(N_DP, N_TABLE, span)
    score = occupied.astype(jnp.int32) * span + mixing
    order = jnp.argsort(-score, axis=-1, stable=True)
    ranked = jnp.argsort(order, axis=-1, stable=True).astype(jnp.int32)
    hot_tab = jax.random.randint(jax.random.fold_in(key, 4), (N_DP, N_TABLE, 1), 0, N_TABLE).astype(jnp.int32)
    spread_tab = jnp.maximum(ranked - CAP_T, 0) % (N_TABLE - 1)
    other_tab = spread_tab + (spread_tab >= hot_tab).astype(jnp.int32)
    grid = jnp.where(ranked < CAP_T, hot_tab, other_tab).astype(jnp.int32)
    source = jnp.arange(devices, dtype=jnp.int32)
    src_dp = jnp.broadcast_to((source // N_TABLE)[:, None], (devices, U_DEV))
    src_tab = jnp.broadcast_to((source % N_TABLE)[:, None], (devices, U_DEV))
    table_of = grid[dp_of, src_tab, src_dp * CAP_DP + place]
    return (dp_of * N_TABLE + table_of).reshape(ALL_UNIQUE).astype(jnp.int32)


def draw_item_rows(key, part):
    key = jax.random.fold_in(key, 7)
    devices = N_DP * N_TABLE
    base = jnp.clip(jax.random.normal(key, (devices, U_DEV, D), jnp.float32), -6.0, 6.0) * D ** (-0.5)
    return base.reshape(ALL_UNIQUE, D).astype(jnp.bfloat16)


def draw_queries(key, part):
    key = jax.random.fold_in(key, 9)
    devices = N_DP * N_TABLE
    base = jnp.clip(jax.random.normal(key, (devices, Q_DEV, D), jnp.float32), -6.0, 6.0) * D ** (-0.5)
    return base.reshape(QUERIES, D).astype(jnp.bfloat16)


def place_ends(entries, own_key, least, high):
    longest = entries.shape.index(max(entries.shape))
    spots = []
    for shift in (0, 1):
        where = [jax.random.randint(jax.random.fold_in(own_key, axis), (), 0, length) for axis, length in enumerate(entries.shape)]
        where[longest] = (where[longest] + shift) % entries.shape[longest]
        spots.append(tuple(where))
    return entries.at[spots[0]].set(least).at[spots[1]].set(high)


def bell_draw(own_key, shape, width, bound, kind=jnp.bfloat16):
    values = jax.random.normal(own_key, shape, jnp.float32) * width
    return jnp.minimum(jnp.maximum(values, -bound), bound).astype(kind)


def setup_inputs(seed: int = 0) -> dict:
    arg_keys = jax.random.split(jax.random.key(seed), 11)
    return {
        "queries": draw_queries(jax.random.fold_in(arg_keys[10], 71), 0),
        "item_rows": draw_item_rows(jax.random.fold_in(arg_keys[10], 71), 0),
        "item_bin": place_ends(jax.random.randint(arg_keys[2], (ALL_UNIQUE,), 0, BINS), jax.random.fold_in(arg_keys[2], 1), 0, BINS - 1).astype(jnp.int32),
        "counts": draw_counts(jax.random.fold_in(arg_keys[10], 71), 0),
        "labels": draw_labels(jax.random.fold_in(arg_keys[10], 71), 0),
        "owner": draw_owner(jax.random.fold_in(arg_keys[10], 71), 0),
        "local_row": place_ends(jax.random.randint(arg_keys[6], (ALL_UNIQUE,), 0, ROWS_DEV), jax.random.fold_in(arg_keys[6], 1), 0, ROWS_DEV - 1).astype(jnp.int32),
        "logq": jnp.clip(jax.random.uniform(arg_keys[7], (BINS,), jnp.float32, -6.0, 0.0), -6.0, 0.0),
        "tower_weight": bell_draw(arg_keys[8], (D, D), D ** -0.5, 0.375),
        "tower_gain": jnp.clip(1.0 + 0.15 * jax.random.normal(arg_keys[9], (D,), jnp.float32), 0.25, 1.75),
    }


NEG = -1.0e30
TEMP = 0.05


def lookup(bins, logq):
    hits = bins[:, None] == jnp.arange(logq.shape[0], dtype=jnp.int32)[None, :]
    return jnp.sum(jnp.where(hits, logq[None, :], jnp.float32(0.0)), axis=1)


def group_grads(packed, logq):
    group_q, group_v, bins, cnt, labs = packed
    slot = jnp.arange(group_v.shape[0], dtype=jnp.int32)
    live = (slot % U_DEV) < jnp.repeat(cnt, U_DEV, total_repeat_length=group_v.shape[0])
    scores = jnp.dot(group_q, group_v.T, preferred_element_type=jnp.float32) / TEMP - lookup(bins, logq)[None, :]
    scores = jnp.where(live[None, :], scores, NEG)
    top = jnp.max(scores, axis=1, keepdims=True)
    weight = jnp.exp(scores - top)
    prob = weight / jnp.sum(weight, axis=1, keepdims=True)
    query = jnp.arange(group_q.shape[0], dtype=jnp.int32)
    target = (query // Q_DEV) * U_DEV + labs
    onehot = (slot[None, :] == target[:, None]).astype(jnp.float32)
    logit_grad = ((prob - onehot) / TEMP).astype(jnp.bfloat16)
    grad_q = jnp.dot(logit_grad, group_v, preferred_element_type=jnp.float32).astype(jnp.bfloat16)
    grad_i = jnp.dot(logit_grad.T, group_q, preferred_element_type=jnp.float32)
    return grad_q, grad_i


def by_group(array, per):
    rest = array.shape[1:]
    moved = array.reshape((N_DP, N_TABLE, per) + rest)
    moved = jnp.swapaxes(moved, 0, 1)
    return moved.reshape((N_TABLE, N_DP * per) + rest)


def from_group(array, per):
    rest = array.shape[2:]
    moved = array.reshape((N_TABLE, N_DP, per) + rest)
    moved = jnp.swapaxes(moved, 0, 1)
    return moved.reshape((N_DP * N_TABLE * per,) + rest)


def reference(queries, item_rows, item_bin, counts, labels, owner, local_row, logq, tower_weight, tower_gain):
    rows_f = item_rows.astype(jnp.float32)
    items = (tower_gain[None, :] * rows_f + jnp.dot(item_rows, tower_weight, preferred_element_type=jnp.float32)).astype(jnp.bfloat16)
    cnt = counts.reshape(N_DP, N_TABLE).T
    packed = (by_group(queries, Q_DEV), by_group(items, U_DEV), by_group(item_bin, U_DEV), cnt, by_group(labels, Q_DEV))
    grad_q, grad_i = lax.map(lambda one: group_grads(one, logq), packed)
    grad_query = from_group(grad_q, Q_DEV)
    item_grad = from_group(grad_i, U_DEV)
    item_grad_b = item_grad.astype(jnp.bfloat16)
    grad_weight = jnp.dot(item_rows.T, item_grad_b, preferred_element_type=jnp.float32) / QUERIES
    grad_gain = jnp.sum(item_grad * rows_f, axis=0) / QUERIES
    row_grad = (tower_gain[None, :] * item_grad + jnp.dot(item_grad_b, tower_weight.T, preferred_element_type=jnp.float32)).astype(jnp.bfloat16)
    dest = owner.astype(jnp.int32) * ROWS_DEV + local_row
    grad_table = jnp.zeros((TABLE_ROWS, D), jnp.float32).at[dest].add(row_grad.astype(jnp.float32))
    return grad_query, grad_table, grad_weight, grad_gain
```

```python
import functools
import math

import jax
import jax.numpy as jnp
from jax import lax
from jax.experimental import pallas as pl
from jax.experimental.pallas import tpu as pltpu
from jax.sharding import PartitionSpec as P

ROWS_DEV = 2048
NEG = -1e30
INV_TEMP = 20.0
SCALE2 = INV_TEMP * math.log2(math.e)
EXT = 16
CORES = 2
X_CHIPS = 4
MESH = pl.DeviceIdType.MESH
F32 = jnp.float32
BF16 = jnp.bfloat16


def iota(shape, dim):
    return lax.broadcasted_iota(jnp.int32, shape, dim)


def dot(a, b, da=1, db=0):
    return lax.dot_general(a, b, (((da,), (db,)), ((), ())), preferred_element_type=F32)


def split3(x):
    hi = x.astype(BF16).astype(F32)
    mid = (x - hi).astype(BF16).astype(F32)
    low = (x - hi - mid).astype(BF16).astype(F32)
    return hi, mid, low


def step_kernel(
    n_dp, n_x, n_z, cap_dp, cap_t,
    q_hbm, rows_hbm, bin_hbm, cnt_hbm, lab_hbm, own_hbm, loc_hbm, logq_hbm, w_hbm, gain_hbm,
    gq_hbm, got_hbm, code_hbm, gw_hbm, gg_hbm,
    q_ref, rows_ref, bin_ref, cnt_ref, lab_ref, own_ref, loc_ref, logq_ref, w_ref, gain_ref,
    gq_ref, got_ref, code_ref, gw_ref, gg_ref,
    blocks, weights, q_t, z_t, top, total, acc, sib_out, sib_in, ring_out, ring_in,
    mid_meta, base_ref, place, first, mid, second, got, meta_out, meta_in,
    w_out, w_in, x_in, r_out, r_in, row_in, full,
    in_sem, out_sem,
    ag_ring_send, ag_ring_recv, ag_sib_send, ag_sib_recv, rs_sib_send, rs_sib_recv, rs_ring_send, rs_ring_recv,
    all_send, all_recv,
):
    n_tab = n_x * n_z
    n_y = n_dp // CORES
    half = n_y // 2
    u_rows, width = rows_ref.shape
    q_rows = q_ref.shape[0]
    queries_all = q_rows * n_dp * n_tab
    cut = u_rows // 2 + EXT
    subs = (pl.ds(0, cut), pl.ds(cut, u_rows + EXT - cut))
    halves = (pl.ds(0, u_rows // 2), pl.ds(u_rows // 2, u_rows // 2))

    fetches = [
        pltpu.make_async_copy(src, dst, in_sem.at[k])
        for k, (src, dst) in enumerate((
            (rows_hbm, rows_ref), (w_hbm, w_ref), (gain_hbm, gain_ref), (bin_hbm, bin_ref),
            (cnt_hbm, cnt_ref), (own_hbm, own_ref), (loc_hbm, loc_ref), (logq_hbm, logq_ref),
            (q_hbm, q_ref), (lab_hbm, lab_ref),
        ))
    ]
    for fetch in fetches:
        fetch.start()

    me, t = lax.axis_index("dp"), lax.axis_index("table")
    y, c = lax.div(me, CORES), lax.rem(me, CORES)
    x, z = lax.div(t, n_z), lax.rem(t, n_z)
    sib = y * CORES + (1 - c)

    def at(y_pos, core):
        return lax.rem(y_pos + 2 * n_y, n_y) * CORES + core

    up, down = at(y + 1, c), at(y - 1, c)

    def turns(n):
        return [(i + 1) // 2 * (1 if i % 2 else -1) for i in range(n)]

    def dp_each(do):
        for off in turns(n_y):
            y_pos = lax.rem(y + (off + n_y), n_y) * CORES
            if off:
                do(y_pos + c)
            do(y_pos + (1 - c))

    def z_each(do):
        for off in turns(n_z)[1:]:
            do(lax.rem(z + (off + n_z), n_z))

    def x_each(do):
        for off in range(1, n_x):
            do(lax.rem(x + off, n_x))

    def tab_each(do):
        cols = [lax.rem(x + off, n_x) * n_z for off in range(n_x)]
        far = lax.rem(z + n_z // 2, n_z)
        for k, col in enumerate(cols):
            if k:
                do(col + z)
            do(col + far)

        def pair(m, _):
            ahead, behind = lax.rem(z + m, n_z), lax.rem(z + n_z - m, n_z)
            for col in cols:
                do(col + ahead)
                do(col + behind)
            return 0

        lax.fori_loop(1, n_z // 2, pair, 0)

    barrier = pltpu.get_barrier_semaphore()

    def greet(axis):
        return lambda peer: pl.semaphore_signal(
            barrier, inc=1, device_id={axis: peer}, device_id_type=MESH
        )

    dp_each(greet("dp"))
    tab_each(greet("table"))

    for fetch in fetches[:8]:
        fetch.wait()
    rows = rows_ref[...]
    blocks[me, :u_rows, :] = rows
    offs = split3(logq_ref[...] * (-1.0 / INV_TEMP))
    table = jnp.zeros((EXT, logq_ref.shape[1]), F32)
    for k, part in enumerate(offs):
        table = jnp.where(iota(table.shape, 0) == k, part, table)
    hits = (iota((logq_ref.shape[1], u_rows), 0) == bin_ref[...]).astype(F32).astype(BF16)
    ext = dot(table.astype(BF16), hits)
    line = iota(ext.shape, 0)
    dead = iota(ext.shape, 1) >= cnt_ref[...]
    ext = jnp.where(dead, jnp.where(line == 0, NEG, 0.0), ext)
    own, loc = own_ref[...], loc_ref[...]
    bits = n_tab.bit_length() - 1
    fields = (own >> bits, own & (n_tab - 1), loc >> 8, loc & 255)
    for k, part in enumerate(fields):
        ext = jnp.where(line == 3 + k, part.astype(F32), ext)
    blocks[me, u_rows:, :] = ext.astype(BF16)
    for fetch in fetches[8:]:
        fetch.wait()
    q_t[...] = q_ref[...].astype(F32).T.astype(BF16)
    z_t[...] = jnp.zeros_like(z_t)
    ring_in[1, 0, 1] = jnp.zeros((u_rows // 2, width), BF16)
    ring_in[0, 0, 0] = jnp.zeros((u_rows // 2, width), BF16)
    base_ref[...] = jnp.zeros_like(base_ref)

    before = (iota((u_rows, u_rows), 0) < iota((u_rows, u_rows), 1)).astype(F32).astype(BF16)
    own_dp = ext[3:4, :]
    is_dp = (iota((n_dp, u_rows), 0).astype(F32) == own_dp).astype(F32)
    rank = jnp.sum(is_dp * dot(is_dp.astype(BF16), before), axis=0, keepdims=True)
    pos = (own_dp * cap_dp + rank).astype(jnp.int32)
    place[...] = (iota((n_dp * cap_dp, u_rows), 0) == pos).astype(F32).astype(BF16)
    pl.semaphore_wait(barrier, n_dp + n_tab - 2)

    def ring_block(b, sub, d, way):
        return pltpu.make_async_remote_copy(
            src_ref=blocks.at[b, subs[sub]], dst_ref=blocks.at[b, subs[sub]],
            send_sem=ag_ring_send.at[way, d, sub], recv_sem=ag_ring_recv.at[b, sub],
            device_id={"dp": up if way else down}, device_id_type=MESH,
        )

    def to_sib(b):
        return pltpu.make_async_remote_copy(
            src_ref=blocks.at[b], dst_ref=blocks.at[b],
            send_sem=ag_sib_send.at[lax.div(b, CORES)], recv_sem=ag_sib_recv.at[lax.div(b, CORES)],
            device_id={"dp": sib}, device_id_type=MESH,
        )

    pick = (iota((EXT, q_rows), 0) < 3).astype(F32).astype(BF16)

    def score(b):
        rows = blocks[b, :u_rows, :]
        items = (gain_ref[...] * rows.astype(F32) + dot(rows, w_ref[...])).astype(BF16)
        raw = dot(items, q_t[...]) + dot(blocks[b, u_rows:, :], pick, 0, 0)
        high = jnp.max(raw, axis=0, keepdims=True)
        e = jnp.exp2((raw - high) * SCALE2)
        weights[b] = e
        top[b] = high
        total[b] = jnp.sum(e, axis=0, keepdims=True)

    def gather_step(d, _):
        near = (at(y + d, c), at(y - d, c))
        between = (d > 0) & (d < half)
        for sub in (0, 1):
            for way in (1, 0):
                b = near[way]

                @pl.when(between | ((d == half) & (sub == 1 - way)))
                def _():
                    ring_block(b, sub, 0, way).wait_recv()

                forward = d < half if sub == 1 - way else d < half - 1

                @pl.when(forward)
                def _():
                    ring_block(b, sub, d, way).start()

        to_sib(near[1]).start()

        @pl.when(between)
        def _():
            to_sib(near[0]).start()

        n = jnp.where((d == 0) | (d == half), 1, 2)

        def one(i, _):
            side, j = lax.div(i, n), lax.rem(i, n)
            b = at(y + (2 * j - 1) * d, jnp.where(side == 0, c, 1 - c))

            @pl.when(side == 1)
            def _():
                to_sib(b).wait_recv()

            score(b)
            return 0

        return lax.fori_loop(0, 2 * n, one, 0)

    lax.fori_loop(0, half + 1, gather_step, 0)

    high = jnp.max(top[...], axis=0)
    rel = jnp.exp2((top[...] - high[None]) * SCALE2)
    mass = jnp.sum(total[...] * rel, axis=0)
    top[...] = rel * (INV_TEMP / mass)[None]

    def sib_copy(slot):
        return pltpu.make_async_remote_copy(
            src_ref=sib_out.at[slot], dst_ref=sib_in.at[slot],
            send_sem=rs_sib_send.at[slot], recv_sem=rs_sib_recv.at[slot],
            device_id={"dp": sib}, device_id_type=MESH,
        )

    def ring_sum(way, k, sub):
        return pltpu.make_async_remote_copy(
            src_ref=ring_out.at[way, k, sub], dst_ref=ring_in.at[way, k, sub],
            send_sem=rs_ring_send.at[way, k, sub], recv_sem=rs_ring_recv.at[way, k, sub],
            device_id={"dp": up if way else down}, device_id_type=MESH,
        )

    def part_of(b):
        lab = jnp.where(b == me, lab_ref[...], -1)
        grad = weights[b] * top[b]
        grad = jnp.where(iota(grad.shape, 0) == lab, grad - INV_TEMP, grad).astype(BF16)
        z_t[...] += dot(blocks[b, :u_rows, :], grad, 0, 0)
        return dot(grad, q_ref[...])

    def event(e, core):
        d, j = half - lax.div(e + 1, 2), lax.rem(e + 1, 2)
        return at(y + (2 * j - 1) * d, core)

    def give_sib(e, _):
        sib_out[e] = part_of(event(e, 1 - c)).astype(BF16)
        sib_copy(e).start()
        return 0

    def take(e):
        part = part_of(event(e, c))
        sib_copy(e).wait_recv()
        return part + sib_in[e].astype(F32)

    DP, TAB, META, W, X, R, ROW, FULL = range(8)

    def send(kind, axis, peer, src, dst):
        pltpu.make_async_remote_copy(
            src_ref=src, dst_ref=dst, send_sem=all_send.at[kind], recv_sem=all_recv.at[kind],
            device_id={axis: peer}, device_id_type=MESH,
        ).start()

    def whole(kind, buf):
        part = buf.at[pl.ds(0, buf.shape[0] - 1)]
        return pltpu.make_async_remote_copy(
            src_ref=part, dst_ref=part, send_sem=all_send.at[kind], recv_sem=all_recv.at[kind],
            device_id={"dp": sib}, device_id_type=MESH,
        )

    me_f = me.astype(F32)
    per = 128 // cap_dp
    n_groups = n_dp // per
    tab_line = iota((n_tab, u_rows), 0).astype(F32)
    spot = iota((128, u_rows), 0).astype(F32)
    ext_line = iota((EXT, u_rows), 0)

    def arrivals(g, _):
        def one(i, carry):
            base, found = carry
            slot = blocks[g * per + i, u_rows:, :].astype(F32)
            here = (slot[3:4, :] == me_f).astype(F32)
            tab, row_hi, row_lo = slot[4:5, :], slot[5:6, :], slot[6:7, :]
            is_tab = jnp.where(tab_line == tab, here, 0.0)
            earlier = dot(is_tab.astype(BF16), before)
            order = jnp.sum(is_tab * (earlier + base), axis=0, keepdims=True)
            nth = jnp.sum(earlier, axis=0, keepdims=True) + (i * cap_dp).astype(F32)
            base = base + jnp.sum(is_tab, axis=1, keepdims=True)
            meta = jnp.zeros((EXT, u_rows), F32)
            for k, part in enumerate((here, tab, order, row_hi, row_lo)):
                meta = jnp.where(ext_line == k, part * here, meta)
            sel = jnp.where(spot == nth, here, 0.0)
            return base, found + dot(meta.astype(BF16), sel.astype(BF16), 1, 1)

        base, found = lax.fori_loop(0, per, one, (base_ref[...], jnp.zeros((EXT, 128), F32)))
        base_ref[...] = base
        mid_meta[:, pl.ds(pl.multiple_of(g * 128, 128), 128)] = found
        return 0

    def ring_step(k):
        for sub in (0, 1):
            for way in (1, 0):
                if k > 1 or sub == 1 - way:
                    ring_sum(way, k - 1, sub).wait_recv()
                so_far = acc[2 * k - 1 + way, halves[sub], :] + ring_in[way, k - 1, sub].astype(F32)
                ring_out[way, k, sub] = so_far.astype(BF16)
                ring_sum(way, k, sub).start()

    def keep(e, _):
        acc[e] = take(e)
        return 0

    give_sib(0, 0)
    far = take(0).astype(BF16)
    for way in (1, 0):
        ring_out[way, 0, 1 - way] = far[halves[1 - way].start : halves[1 - way].start + u_rows // 2]
        ring_sum(way, 0, 1 - way).start()
    lax.fori_loop(1, n_y, give_sib, 0)
    early = 1
    if half > 1:
        early = 3
        lax.fori_loop(1, early, keep, 0)
        ring_step(1)
    lax.fori_loop(early, n_y, keep, 0)

    z_hi = z_t[...].astype(BF16)
    z_low = (z_t[...] - z_hi.astype(F32)).astype(BF16)
    w_out[...] = (dot(z_hi, q_ref[...]) + dot(z_low, q_ref[...])).astype(BF16).reshape(w_out.shape)
    z_each(lambda p: send(W, "table", x * n_z + p, w_out.at[p], w_in.at[z]))
    w_in[z] = w_out[z]

    def sum_z():
        whole(W, w_in).wait_recv()
        x_in[x] = jnp.sum(w_in[...].astype(F32), axis=0)
        x_each(lambda p: send(X, "table", p * n_z + z, x_in.at[x], x_in.at[x]))

    def sum_x():
        whole(X, x_in).wait_recv()
        r_out[...] = jnp.sum(x_in[...], axis=0).reshape(r_out.shape)
        dp_each(lambda p: send(R, "dp", p, r_out.at[p], r_in.at[me]))
        r_in[me] = r_out[me]

    def some(first_group, last_group):
        lax.fori_loop(first_group, last_group, arrivals, 0)

    work = [
        lambda: (some(0, n_groups // 2), sum_z()),
        lambda: (some(n_groups // 2, n_groups), sum_x()),
    ]
    for k in range(2, half):
        ring_step(k)
        if work:
            work.pop(0)()
    for do in work:
        do()

    for sub in (0, 1):
        for way in (1, 0):
            if sub == 1 - way or half > 1:
                ring_sum(way, half - 1, sub).wait_recv()
    for sub in (0, 1):
        arrived = ring_in[0, half - 1, sub].astype(F32) + ring_in[1, half - 1, sub].astype(F32)
        acc[n_y - 1, halves[sub], :] += arrived
    ig = acc[n_y - 1]
    row_grad = (gain_ref[...] * ig + dot(ig.astype(BF16), w_ref[...], 1, 1)).astype(BF16)
    first[...] = dot(place[...], row_grad).astype(BF16).reshape(first.shape)
    dp_each(lambda p: send(DP, "dp", p, first.at[p], mid.at[me]))
    mid[me] = first[me]

    n_mid = n_dp * cap_dp
    meta = mid_meta[...]
    valid, tab, order, row_hi, row_lo = (meta[k : k + 1, :] for k in range(5))
    tab = jnp.where(valid > 0.5, tab, -1.0)
    is_tab = iota((n_tab, n_mid), 0).astype(F32) == tab
    is_order = (iota((128, n_mid), 0).astype(F32) == order).astype(F32).astype(BF16)

    def spread(value):
        return dot(jnp.where(is_tab, value, 0.0).astype(BF16), is_order, 1, 1)

    code = 256.0 * spread(row_hi) + spread(row_lo) + spread(valid) - 1.0
    meta_out[...] = code.reshape(meta_out.shape)
    tab_each(lambda p: send(META, "table", p, meta_out.at[p], meta_in.at[t]))
    meta_in[t] = meta_out[t]

    whole(R, r_in).wait_recv()
    row_in[me] = jnp.sum(r_in[...], axis=0) * (1.0 / queries_all)
    dp_each(lambda p: send(ROW, "dp", p, row_in.at[me], row_in.at[me]))

    pos2 = (tab * cap_t + order).astype(jnp.int32)
    place2 = (iota((n_tab * cap_t, n_mid), 0) == pos2).astype(F32).astype(BF16)

    whole(DP, mid).wait_recv()
    out = dot(place2, mid[...].reshape(n_mid, width)).reshape(n_tab, cap_t, width)
    second[:, :cap_t, :] = out[:, :, :128].astype(BF16)
    second[:, cap_t:, :] = out[:, :, 128:].astype(BF16)
    tab_each(lambda p: send(TAB, "table", p, second.at[p], got.at[t]))
    got[t] = second[t]

    whole(ROW, row_in).wait_recv()
    full[z] = row_in[...]
    z_each(lambda p: send(FULL, "table", x * n_z + p, full.at[z], full.at[z]))

    z_all = z_t[...].T
    z_hi = z_all.astype(BF16)
    z_low = (z_all - z_hi.astype(F32)).astype(BF16)
    gq_ref[...] = (gain_ref[...] * z_all + dot(z_hi, w_ref[...]) + dot(z_low, w_ref[...])).astype(BF16)
    gq_copy = pltpu.make_async_copy(gq_ref, gq_hbm, out_sem.at[0])
    gq_copy.start()

    whole(META, meta_in).wait_recv()
    code = meta_in[...].reshape(n_tab, 128).astype(jnp.int32) + 1
    n_got = n_tab * cap_t
    cols = iota((1, n_got), 1)
    is_src = (iota((n_tab, n_got), 0) == lax.div(iota((n_tab, n_got), 1), cap_t)).astype(F32).astype(BF16)

    def along(value):
        return dot(value.astype(F32).astype(BF16), is_src, 0, 0)

    wide = 256.0 * along(code >> 8) + along(code & 255) - 1.0
    mine = iota((128, n_got), 0) == lax.rem(cols, cap_t)
    code_ref[...] = jnp.sum(jnp.where(mine, wide, 0.0), axis=0, keepdims=True).astype(jnp.int32)
    code_copy = pltpu.make_async_copy(code_ref, code_hbm, out_sem.at[1])
    code_copy.start()

    for d in range(half):
        for way in (0, 1):
            for sub in (0, 1):
                if sub == 1 - way or d < half - 1:
                    ring_block(me, sub, d, way).wait_send()
                if sub == 1 - way or d > 0:
                    ring_sum(way, d, sub).wait_send()
    for k in range(n_y):
        to_sib(k * CORES).wait_send()
        sib_copy(k).wait_send()
    for kind, buf in ((W, w_in), (X, x_in), (R, r_in), (ROW, row_in), (META, meta_in), (DP, mid)):
        whole(kind, buf).wait_send()

    whole(FULL, full).wait_recv()
    gw = full[...].reshape(width, width)
    gw_ref[...] = gw
    gw_copy = pltpu.make_async_copy(gw_ref, gw_hbm, out_sem.at[2])
    gw_copy.start()
    diag = iota((width, width), 0) == iota((width, width), 1)
    gg_ref[...] = jnp.sum(jnp.where(diag, gw, 0.0), axis=0, keepdims=True)
    gg_copy = pltpu.make_async_copy(gg_ref, gg_hbm, out_sem.at[3])
    gg_copy.start()

    whole(TAB, got).wait_recv()
    arrived = got[...].astype(F32)
    got_ref[:, :128] = arrived[:, :cap_t, :].reshape(n_got, 128).astype(BF16)
    got_ref[:, 128:] = arrived[:, cap_t:, :].reshape(n_got, 128).astype(BF16)
    got_copy = pltpu.make_async_copy(got_ref, got_hbm, out_sem.at[4])
    got_copy.start()
    whole(TAB, got).wait_send()
    whole(FULL, full).wait_send()
    for copy in (gq_copy, code_copy, gw_copy, gg_copy, got_copy):
        copy.wait()


def step(n_dp, n_x, n_z, queries, item_rows, item_bin, counts, labels, owner, local_row, logq, w, gain):
    q_rows, width = queries.shape
    u_rows = item_rows.shape[0]
    n_tab = n_x * n_z
    n_y = n_dp // CORES
    half = n_y // 2
    cap_dp = max(2, 2 * u_rows // n_dp)
    cap_t = max(2, (n_dp * cap_dp + n_tab - 1) // n_tab)
    z_rows = width // n_z
    r_rows = z_rows // n_dp
    args = (
        queries, item_rows, item_bin[None], counts[None], labels[None], owner[None], local_row[None],
        logq[None], w, gain[None],
    )
    outs = (
        jax.ShapeDtypeStruct((q_rows, width), BF16),
        jax.ShapeDtypeStruct((n_tab * cap_t, width), BF16),
        jax.ShapeDtypeStruct((1, n_tab * cap_t), jnp.int32),
        jax.ShapeDtypeStruct((width, width), F32),
        jax.ShapeDtypeStruct((1, width), F32),
    )
    vmem = pltpu.VMEM
    sem = pltpu.SemaphoreType.DMA
    return pl.pallas_call(
        functools.partial(step_kernel, n_dp, n_x, n_z, cap_dp, cap_t),
        out_shape=outs,
        in_specs=[pl.BlockSpec(memory_space=pl.ANY)] * len(args),
        out_specs=(pl.BlockSpec(memory_space=pl.ANY),) * len(outs),
        scratch_shapes=[vmem(a.shape, a.dtype) for a in args + outs]
        + [
            vmem((n_dp, u_rows + EXT, width), BF16),
            vmem((n_dp, u_rows, q_rows), F32),
            vmem((width, q_rows), BF16),
            vmem((width, q_rows), F32),
            vmem((n_dp, 1, q_rows), F32),
            vmem((n_dp, 1, q_rows), F32),
            vmem((n_y, u_rows, width), F32),
            vmem((n_y, u_rows, width), BF16),
            vmem((n_y, u_rows, width), BF16),
            vmem((2, half, 2, u_rows // 2, width), BF16),
            vmem((2, half, 2, u_rows // 2, width), BF16),
            vmem((EXT, n_dp * cap_dp), F32),
            vmem((n_tab, 1), F32),
            vmem((n_dp * cap_dp, u_rows), BF16),
            vmem((n_dp, cap_dp, width), BF16),
            vmem((n_dp, cap_dp, width), BF16),
            vmem((n_tab, 2 * cap_t, 128), BF16),
            vmem((n_tab, 2 * cap_t, 128), BF16),
            vmem((n_tab, 1, 128), F32),
            vmem((n_tab, 1, 128), F32),
            vmem((n_z, z_rows, width), BF16),
            vmem((n_z, z_rows, width), BF16),
            vmem((n_x, z_rows, width), F32),
            vmem((n_dp, r_rows, width), F32),
            vmem((n_dp, r_rows, width), F32),
            vmem((n_dp, r_rows, width), F32),
            vmem((n_z, n_dp, r_rows, width), F32),
            sem((len(args),)), sem((len(outs),)),
            sem((2, half, 2)), sem((n_dp, 2)), sem((n_y,)), sem((n_y,)),
            sem((n_y,)), sem((n_y,)), sem((2, half, 2)), sem((2, half, 2)),
            sem((8,)), sem((8,)),
        ],
        compiler_params=pltpu.CompilerParams(
            collective_id=0, has_side_effects=True, vmem_limit_bytes=60 << 20
        ),
        name="group_step",
    )(*args)


def place_kernel(got_ref, code_ref, gq_in, gw_in, gg_in, out_ref, gq_ref, gw_ref, gg_ref):
    tile = out_ref.shape[0]
    line = iota((tile, code_ref.shape[1]), 0) + pl.program_id(0) * tile
    hits = (line == code_ref[...]).astype(F32).astype(BF16)
    out_ref[...] = dot(hits, got_ref[...])

    @pl.when(pl.program_id(0) == 0)
    def _():
        gq_ref[...] = gq_in[...]
        gw_ref[...] = gw_in[...]
        gg_ref[...] = gg_in[...]


def place_rows(got, code, *others):
    tile = 512
    n_got, width = got.shape
    whole = lambda a: pl.BlockSpec(a.shape, lambda i: (0, 0))
    return pl.pallas_call(
        place_kernel,
        grid=(ROWS_DEV // tile,),
        out_shape=(jax.ShapeDtypeStruct((ROWS_DEV, width), F32),)
        + tuple(jax.ShapeDtypeStruct(a.shape, a.dtype) for a in others),
        in_specs=[whole(a) for a in (got, code, *others)],
        out_specs=(pl.BlockSpec((tile, width), lambda i: (i, 0)),) + tuple(whole(a) for a in others),
        compiler_params=pltpu.CompilerParams(vmem_limit_bytes=32 << 20),
        name="place_rows",
    )(got, code, *others)


def body(n_dp, n_x, n_z, *args):
    grad_query, got, code, gw, gg = step(n_dp, n_x, n_z, *args)
    grad_table, grad_query, gw, gg = place_rows(got, code, grad_query, gw, gg)
    return grad_query, grad_table, gw, gg.reshape(-1)


def solution(mesh):
    n_x = X_CHIPS
    split = P(("dp", "table"))
    split2 = P(("dp", "table"), None)
    return jax.shard_map(
        functools.partial(body, mesh.shape["dp"], n_x, mesh.shape["table"] // n_x),
        mesh=mesh,
        in_specs=(split2, split2, split, split, split, split, split, P(), P(), P()),
        out_specs=(split2, split2, P(), P()),
        check_vma=False,
    )
```

```python
import functools
import math

import jax
import jax.numpy as jnp
from jax import lax
from jax.experimental import pallas as pl
from jax.experimental.pallas import tpu as pltpu
from jax.sharding import PartitionSpec as P

ROWS_DEV = 2048
NEG = -1e30
INV_TEMP = 20.0
SCALE2 = INV_TEMP * math.log2(math.e)
EXT = 16
CORES = 2
X_CHIPS = 4
MESH = pl.DeviceIdType.MESH
F32 = jnp.float32
BF16 = jnp.bfloat16


def iota(shape, dim):
    return lax.broadcasted_iota(jnp.int32, shape, dim)


def dot(a, b, da=1, db=0):
    return lax.dot_general(a, b, (((da,), (db,)), ((), ())), preferred_element_type=F32)


def split3(x):
    hi = x.astype(BF16).astype(F32)
    mid = (x - hi).astype(BF16).astype(F32)
    low = (x - hi - mid).astype(BF16).astype(F32)
    return hi, mid, low


def step_kernel(
    n_dp, n_x, n_z, cap_dp, cap_t,
    q_hbm, rows_hbm, bin_hbm, cnt_hbm, lab_hbm, own_hbm, loc_hbm, logq_hbm, w_hbm, gain_hbm,
    gq_hbm, got_hbm, code_hbm, gw_hbm, gg_hbm,
    q_ref, rows_ref, bin_ref, cnt_ref, lab_ref, own_ref, loc_ref, logq_ref, w_ref, gain_ref,
    gq_ref, got_ref, code_ref, gw_ref, gg_ref,
    blocks, weights, q_t, z_t, top, total, acc, sib_out, sib_in, ring_out, ring_in,
    mid_meta, base_ref, place, first, mid, second, got, meta_out, meta_in,
    w_out, w_in, x_in, r_out, r_in, row_in, full,
    in_sem, out_sem,
    ag_ring_send, ag_ring_recv, ag_sib_send, ag_sib_recv, rs_sib_send, rs_sib_recv, rs_ring_send, rs_ring_recv,
    all_send, all_recv,
):
    n_tab = n_x * n_z
    n_y = n_dp // CORES
    half = n_y // 2
    u_rows, width = rows_ref.shape
    q_rows = q_ref.shape[0]
    queries_all = q_rows * n_dp * n_tab
    cut = u_rows // 2 + EXT
    subs = (pl.ds(0, cut), pl.ds(cut, u_rows + EXT - cut))
    halves = (pl.ds(0, u_rows // 2), pl.ds(u_rows // 2, u_rows // 2))

    fetches = [
        pltpu.make_async_copy(src, dst, in_sem.at[k])
        for k, (src, dst) in enumerate((
            (rows_hbm, rows_ref), (w_hbm, w_ref), (gain_hbm, gain_ref), (bin_hbm, bin_ref),
            (cnt_hbm, cnt_ref), (own_hbm, own_ref), (loc_hbm, loc_ref), (logq_hbm, logq_ref),
            (q_hbm, q_ref), (lab_hbm, lab_ref),
        ))
    ]
    for fetch in fetches:
        fetch.start()

    me, t = lax.axis_index("dp"), lax.axis_index("table")
    y, c = lax.div(me, CORES), lax.rem(me, CORES)
    x, z = lax.div(t, n_z), lax.rem(t, n_z)
    sib = y * CORES + (1 - c)

    def at(y_pos, core):
        return lax.rem(y_pos + 2 * n_y, n_y) * CORES + core

    up, down = at(y + 1, c), at(y - 1, c)

    def turns(n):
        return [(i + 1) // 2 * (1 if i % 2 else -1) for i in range(n)]

    def dp_each(do):
        for off in turns(n_y):
            y_pos = lax.rem(y + (off + n_y), n_y) * CORES
            if off:
                do(y_pos + c)
            do(y_pos + (1 - c))

    def z_each(do):
        for off in turns(n_z)[1:]:
            do(lax.rem(z + (off + n_z), n_z))

    def x_each(do):
        for off in range(1, n_x):
            do(lax.rem(x + off, n_x))

    def tab_each(do):
        cols = [lax.rem(x + off, n_x) * n_z for off in range(n_x)]
        far = lax.rem(z + n_z // 2, n_z)
        for k, col in enumerate(cols):
            if k:
                do(col + z)
            do(col + far)

        def pair(m, _):
            ahead, behind = lax.rem(z + m, n_z), lax.rem(z + n_z - m, n_z)
            for col in cols:
                do(col + ahead)
                do(col + behind)
            return 0

        lax.fori_loop(1, n_z // 2, pair, 0)

    barrier = pltpu.get_barrier_semaphore()

    def greet(axis):
        return lambda peer: pl.semaphore_signal(
            barrier, inc=1, device_id={axis: peer}, device_id_type=MESH
        )

    dp_each(greet("dp"))
    tab_each(greet("table"))

    for fetch in fetches[:8]:
        fetch.wait()
    rows = rows_ref[...]
    blocks[me, :u_rows, :] = rows
    offs = split3(logq_ref[...] * (-1.0 / INV_TEMP))
    table = jnp.zeros((EXT, logq_ref.shape[1]), F32)
    for k, part in enumerate(offs):
        table = jnp.where(iota(table.shape, 0) == k, part, table)
    hits = (iota((logq_ref.shape[1], u_rows), 0) == bin_ref[...]).astype(F32).astype(BF16)
    ext = dot(table.astype(BF16), hits)
    line = iota(ext.shape, 0)
    dead = iota(ext.shape, 1) >= cnt_ref[...]
    ext = jnp.where(dead, jnp.where(line == 0, NEG, 0.0), ext)
    own, loc = own_ref[...], loc_ref[...]
    bits = n_tab.bit_length() - 1
    fields = (own >> bits, own & (n_tab - 1), loc >> 8, loc & 255)
    for k, part in enumerate(fields):
        ext = jnp.where(line == 3 + k, part.astype(F32), ext)
    blocks[me, u_rows:, :] = ext.astype(BF16)
    for fetch in fetches[8:]:
        fetch.wait()
    q_t[...] = q_ref[...].astype(F32).T.astype(BF16)
    z_t[...] = jnp.zeros_like(z_t)
    ring_in[1, 0, 1] = jnp.zeros((u_rows // 2, width), BF16)
    ring_in[0, 0, 0] = jnp.zeros((u_rows // 2, width), BF16)
    base_ref[...] = jnp.zeros_like(base_ref)

    before = (iota((u_rows, u_rows), 0) < iota((u_rows, u_rows), 1)).astype(F32).astype(BF16)
    own_dp = ext[3:4, :]
    is_dp = (iota((n_dp, u_rows), 0).astype(F32) == own_dp).astype(F32)
    rank = jnp.sum(is_dp * dot(is_dp.astype(BF16), before), axis=0, keepdims=True)
    pos = (own_dp * cap_dp + rank).astype(jnp.int32)
    place[...] = (iota((n_dp * cap_dp, u_rows), 0) == pos).astype(F32).astype(BF16)
    pl.semaphore_wait(barrier, n_dp + n_tab - 2)

    def ring_block(b, sub, d, way):
        return pltpu.make_async_remote_copy(
            src_ref=blocks.at[b, subs[sub]], dst_ref=blocks.at[b, subs[sub]],
            send_sem=ag_ring_send.at[way, d, sub], recv_sem=ag_ring_recv.at[b, sub],
            device_id={"dp": up if way else down}, device_id_type=MESH,
        )

    def to_sib(b):
        return pltpu.make_async_remote_copy(
            src_ref=blocks.at[b], dst_ref=blocks.at[b],
            send_sem=ag_sib_send.at[lax.div(b, CORES)], recv_sem=ag_sib_recv.at[lax.div(b, CORES)],
            device_id={"dp": sib}, device_id_type=MESH,
        )

    pick = (iota((EXT, q_rows), 0) < 3).astype(F32).astype(BF16)

    def score(b):
        rows = blocks[b, :u_rows, :]
        items = (gain_ref[...] * rows.astype(F32) + dot(rows, w_ref[...])).astype(BF16)
        raw = dot(items, q_t[...]) + dot(blocks[b, u_rows:, :], pick, 0, 0)
        high = jnp.max(raw, axis=0, keepdims=True)
        e = jnp.exp2((raw - high) * SCALE2)
        weights[b] = e
        top[b] = high
        total[b] = jnp.sum(e, axis=0, keepdims=True)

    def gather_step(d, _):
        near = (at(y + d, c), at(y - d, c))
        between = (d > 0) & (d < half)
        for sub in (0, 1):
            for way in (1, 0):
                b = near[way]

                @pl.when(between | ((d == half) & (sub == 1 - way)))
                def _():
                    ring_block(b, sub, 0, way).wait_recv()

                forward = d < half if sub == 1 - way else d < half - 1

                @pl.when(forward)
                def _():
                    ring_block(b, sub, d, way).start()

        to_sib(near[1]).start()

        @pl.when(between)
        def _():
            to_sib(near[0]).start()

        def one(j, _):
            score(at(y + (2 * j - 1) * d, c))
            return 0

        lax.fori_loop(0, ways(d), one, 0)

        @pl.when(d > 0)
        def _():
            from_sib(d - 1)

        return 0

    def ways(d):
        return jnp.where((d == 0) | (d == half), 1, 2)

    def from_sib(d):
        def one(j, _):
            b = at(y + (2 * j - 1) * d, 1 - c)
            to_sib(b).wait_recv()
            score(b)
            return 0

        lax.fori_loop(0, ways(d), one, 0)

    lax.fori_loop(0, half + 1, gather_step, 0)
    from_sib(half)

    high = jnp.max(top[...], axis=0)
    rel = jnp.exp2((top[...] - high[None]) * SCALE2)
    mass = jnp.sum(total[...] * rel, axis=0)
    top[...] = rel * (INV_TEMP / mass)[None]

    def sib_copy(slot):
        return pltpu.make_async_remote_copy(
            src_ref=sib_out.at[slot], dst_ref=sib_in.at[slot],
            send_sem=rs_sib_send.at[slot], recv_sem=rs_sib_recv.at[slot],
            device_id={"dp": sib}, device_id_type=MESH,
        )

    def ring_sum(way, k, sub):
        return pltpu.make_async_remote_copy(
            src_ref=ring_out.at[way, k, sub], dst_ref=ring_in.at[way, k, sub],
            send_sem=rs_ring_send.at[way, k, sub], recv_sem=rs_ring_recv.at[way, k, sub],
            device_id={"dp": up if way else down}, device_id_type=MESH,
        )

    def part_of(b):
        lab = jnp.where(b == me, lab_ref[...], -1)
        grad = weights[b] * top[b]
        grad = jnp.where(iota(grad.shape, 0) == lab, grad - INV_TEMP, grad).astype(BF16)
        z_t[...] += dot(blocks[b, :u_rows, :], grad, 0, 0)
        return dot(grad, q_ref[...])

    def event(e, core):
        d, j = half - lax.div(e + 1, 2), lax.rem(e + 1, 2)
        return at(y + (2 * j - 1) * d, core)

    def give_sib(e, _):
        sib_out[e] = part_of(event(e, 1 - c)).astype(BF16)
        sib_copy(e).start()
        return 0

    def take(e):
        part = part_of(event(e, c))
        sib_copy(e).wait_recv()
        return part + sib_in[e].astype(F32)

    DP, TAB, META, W, X, R, ROW, FULL = range(8)

    def send(kind, axis, peer, src, dst):
        pltpu.make_async_remote_copy(
            src_ref=src, dst_ref=dst, send_sem=all_send.at[kind], recv_sem=all_recv.at[kind],
            device_id={axis: peer}, device_id_type=MESH,
        ).start()

    def whole(kind, buf):
        part = buf.at[pl.ds(0, buf.shape[0] - 1)]
        return pltpu.make_async_remote_copy(
            src_ref=part, dst_ref=part, send_sem=all_send.at[kind], recv_sem=all_recv.at[kind],
            device_id={"dp": sib}, device_id_type=MESH,
        )

    me_f = me.astype(F32)
    per = 128 // cap_dp
    n_groups = n_dp // per
    tab_line = iota((n_tab, u_rows), 0).astype(F32)
    spot = iota((128, u_rows), 0).astype(F32)
    ext_line = iota((EXT, u_rows), 0)

    def arrivals(g, _):
        def one(i, carry):
            base, found = carry
            slot = blocks[g * per + i, u_rows:, :].astype(F32)
            here = (slot[3:4, :] == me_f).astype(F32)
            tab, row_hi, row_lo = slot[4:5, :], slot[5:6, :], slot[6:7, :]
            is_tab = jnp.where(tab_line == tab, here, 0.0)
            earlier = dot(is_tab.astype(BF16), before)
            order = jnp.sum(is_tab * (earlier + base), axis=0, keepdims=True)
            nth = jnp.sum(earlier, axis=0, keepdims=True) + (i * cap_dp).astype(F32)
            base = base + jnp.sum(is_tab, axis=1, keepdims=True)
            meta = jnp.zeros((EXT, u_rows), F32)
            for k, part in enumerate((here, tab, order, row_hi, row_lo)):
                meta = jnp.where(ext_line == k, part * here, meta)
            sel = jnp.where(spot == nth, here, 0.0)
            return base, found + dot(meta.astype(BF16), sel.astype(BF16), 1, 1)

        base, found = lax.fori_loop(0, per, one, (base_ref[...], jnp.zeros((EXT, 128), F32)))
        base_ref[...] = base
        mid_meta[:, pl.ds(pl.multiple_of(g * 128, 128), 128)] = found
        return 0

    def ring_step(k):
        for sub in (0, 1):
            for way in (1, 0):
                if k > 1 or sub == 1 - way:
                    ring_sum(way, k - 1, sub).wait_recv()
                so_far = acc[2 * k - 1 + way, halves[sub], :] + ring_in[way, k - 1, sub].astype(F32)
                ring_out[way, k, sub] = so_far.astype(BF16)
                ring_sum(way, k, sub).start()

    def keep(e, _):
        acc[e] = take(e)
        return 0

    give_sib(0, 0)
    far = take(0).astype(BF16)
    for way in (1, 0):
        ring_out[way, 0, 1 - way] = far[halves[1 - way].start : halves[1 - way].start + u_rows // 2]
        ring_sum(way, 0, 1 - way).start()
    lax.fori_loop(1, n_y, give_sib, 0)
    early = 1
    if half > 1:
        early = 3
        lax.fori_loop(1, early, keep, 0)
        ring_step(1)
    lax.fori_loop(early, n_y, keep, 0)

    z_hi = z_t[...].astype(BF16)
    z_low = (z_t[...] - z_hi.astype(F32)).astype(BF16)
    w_out[...] = (dot(z_hi, q_ref[...]) + dot(z_low, q_ref[...])).astype(BF16).reshape(w_out.shape)
    dp_each(lambda p: send(W, "dp", p, w_out.at[p], w_in.at[me]))
    w_in[me] = w_out[me]

    def sum_dp():
        whole(W, w_in).wait_recv()
        r_out[...] = jnp.sum(w_in[...].astype(F32), axis=0).reshape(r_out.shape)
        z_each(lambda p: send(R, "table", x * n_z + p, r_out.at[p], r_in.at[z]))
        r_in[z] = r_out[z]

    def sum_z():
        whole(R, r_in).wait_recv()
        x_in[x] = jnp.sum(r_in[...], axis=0)
        x_each(lambda p: send(X, "table", p * n_z + z, x_in.at[x], x_in.at[x]))

    def some(first_group, last_group):
        lax.fori_loop(first_group, last_group, arrivals, 0)

    work = [
        lambda: (some(0, n_groups // 2), sum_dp()),
        lambda: (some(n_groups // 2, n_groups), sum_z()),
    ]
    for k in range(2, half):
        ring_step(k)
        if work:
            work.pop(0)()
    for do in work:
        do()

    for sub in (0, 1):
        for way in (1, 0):
            if sub == 1 - way or half > 1:
                ring_sum(way, half - 1, sub).wait_recv()
    for sub in (0, 1):
        arrived = ring_in[0, half - 1, sub].astype(F32) + ring_in[1, half - 1, sub].astype(F32)
        acc[n_y - 1, halves[sub], :] += arrived
    ig = acc[n_y - 1]
    row_grad = (gain_ref[...] * ig + dot(ig.astype(BF16), w_ref[...], 1, 1)).astype(BF16)
    first[...] = dot(place[...], row_grad).astype(BF16).reshape(first.shape)
    dp_each(lambda p: send(DP, "dp", p, first.at[p], mid.at[me]))
    mid[me] = first[me]

    whole(X, x_in).wait_recv()
    row_in[z] = jnp.sum(x_in[...], axis=0) * (1.0 / queries_all)
    z_each(lambda p: send(ROW, "table", x * n_z + p, row_in.at[z], row_in.at[z]))

    n_mid = n_dp * cap_dp
    meta = mid_meta[...]
    valid, tab, order, row_hi, row_lo = (meta[k : k + 1, :] for k in range(5))
    tab = jnp.where(valid > 0.5, tab, -1.0)
    is_tab = iota((n_tab, n_mid), 0).astype(F32) == tab
    is_order = (iota((128, n_mid), 0).astype(F32) == order).astype(F32).astype(BF16)

    def spread(value):
        return dot(jnp.where(is_tab, value, 0.0).astype(BF16), is_order, 1, 1)

    code = 256.0 * spread(row_hi) + spread(row_lo) + spread(valid) - 1.0
    meta_out[...] = code.reshape(meta_out.shape)
    tab_each(lambda p: send(META, "table", p, meta_out.at[p], meta_in.at[t]))
    meta_in[t] = meta_out[t]

    pos2 = (tab * cap_t + order).astype(jnp.int32)
    place2 = (iota((n_tab * cap_t, n_mid), 0) == pos2).astype(F32).astype(BF16)

    whole(DP, mid).wait_recv()
    out = dot(place2, mid[...].reshape(n_mid, width)).reshape(n_tab, cap_t, width)
    second[:, :cap_t, :] = out[:, :, :128].astype(BF16)
    second[:, cap_t:, :] = out[:, :, 128:].astype(BF16)
    tab_each(lambda p: send(TAB, "table", p, second.at[p], got.at[t]))
    got[t] = second[t]

    whole(ROW, row_in).wait_recv()
    full[me] = row_in[...]
    dp_each(lambda p: send(FULL, "dp", p, full.at[me], full.at[me]))

    z_all = z_t[...].T
    z_hi = z_all.astype(BF16)
    z_low = (z_all - z_hi.astype(F32)).astype(BF16)
    gq_ref[...] = (gain_ref[...] * z_all + dot(z_hi, w_ref[...]) + dot(z_low, w_ref[...])).astype(BF16)
    gq_copy = pltpu.make_async_copy(gq_ref, gq_hbm, out_sem.at[0])
    gq_copy.start()

    whole(META, meta_in).wait_recv()
    code = meta_in[...].reshape(n_tab, 128).astype(jnp.int32) + 1
    n_got = n_tab * cap_t
    cols = iota((1, n_got), 1)
    is_src = (iota((n_tab, n_got), 0) == lax.div(iota((n_tab, n_got), 1), cap_t)).astype(F32).astype(BF16)

    def along(value):
        return dot(value.astype(F32).astype(BF16), is_src, 0, 0)

    wide = 256.0 * along(code >> 8) + along(code & 255) - 1.0
    mine = iota((128, n_got), 0) == lax.rem(cols, cap_t)
    code_ref[...] = jnp.sum(jnp.where(mine, wide, 0.0), axis=0, keepdims=True).astype(jnp.int32)
    code_copy = pltpu.make_async_copy(code_ref, code_hbm, out_sem.at[1])
    code_copy.start()

    for d in range(half):
        for way in (0, 1):
            for sub in (0, 1):
                if sub == 1 - way or d < half - 1:
                    ring_block(me, sub, d, way).wait_send()
                if sub == 1 - way or d > 0:
                    ring_sum(way, d, sub).wait_send()
    for k in range(n_y):
        to_sib(k * CORES).wait_send()
        sib_copy(k).wait_send()
    for kind, buf in ((W, w_in), (X, x_in), (R, r_in), (ROW, row_in), (META, meta_in), (DP, mid)):
        whole(kind, buf).wait_send()

    whole(FULL, full).wait_recv()
    gw = full[...].reshape(width, width)
    gw_ref[...] = gw
    gw_copy = pltpu.make_async_copy(gw_ref, gw_hbm, out_sem.at[2])
    gw_copy.start()
    diag = iota((width, width), 0) == iota((width, width), 1)
    gg_ref[...] = jnp.sum(jnp.where(diag, gw, 0.0), axis=0, keepdims=True)
    gg_copy = pltpu.make_async_copy(gg_ref, gg_hbm, out_sem.at[3])
    gg_copy.start()

    whole(TAB, got).wait_recv()
    arrived = got[...].astype(F32)
    got_ref[:, :128] = arrived[:, :cap_t, :].reshape(n_got, 128).astype(BF16)
    got_ref[:, 128:] = arrived[:, cap_t:, :].reshape(n_got, 128).astype(BF16)
    got_copy = pltpu.make_async_copy(got_ref, got_hbm, out_sem.at[4])
    got_copy.start()
    whole(TAB, got).wait_send()
    whole(FULL, full).wait_send()
    for copy in (gq_copy, code_copy, gw_copy, gg_copy, got_copy):
        copy.wait()


def step(n_dp, n_x, n_z, queries, item_rows, item_bin, counts, labels, owner, local_row, logq, w, gain):
    q_rows, width = queries.shape
    u_rows = item_rows.shape[0]
    n_tab = n_x * n_z
    n_y = n_dp // CORES
    half = n_y // 2
    cap_dp = max(2, 2 * u_rows // n_dp)
    cap_t = max(2, (n_dp * cap_dp + n_tab - 1) // n_tab)
    w_rows = width // n_dp
    r_rows = w_rows // n_z
    args = (
        queries, item_rows, item_bin[None], counts[None], labels[None], owner[None], local_row[None],
        logq[None], w, gain[None],
    )
    outs = (
        jax.ShapeDtypeStruct((q_rows, width), BF16),
        jax.ShapeDtypeStruct((n_tab * cap_t, width), BF16),
        jax.ShapeDtypeStruct((1, n_tab * cap_t), jnp.int32),
        jax.ShapeDtypeStruct((width, width), F32),
        jax.ShapeDtypeStruct((1, width), F32),
    )
    vmem = pltpu.VMEM
    sem = pltpu.SemaphoreType.DMA
    return pl.pallas_call(
        functools.partial(step_kernel, n_dp, n_x, n_z, cap_dp, cap_t),
        out_shape=outs,
        in_specs=[pl.BlockSpec(memory_space=pl.ANY)] * len(args),
        out_specs=(pl.BlockSpec(memory_space=pl.ANY),) * len(outs),
        scratch_shapes=[vmem(a.shape, a.dtype) for a in args + outs]
        + [
            vmem((n_dp, u_rows + EXT, width), BF16),
            vmem((n_dp, u_rows, q_rows), F32),
            vmem((width, q_rows), BF16),
            vmem((width, q_rows), F32),
            vmem((n_dp, 1, q_rows), F32),
            vmem((n_dp, 1, q_rows), F32),
            vmem((n_y, u_rows, width), F32),
            vmem((n_y, u_rows, width), BF16),
            vmem((n_y, u_rows, width), BF16),
            vmem((2, half, 2, u_rows // 2, width), BF16),
            vmem((2, half, 2, u_rows // 2, width), BF16),
            vmem((EXT, n_dp * cap_dp), F32),
            vmem((n_tab, 1), F32),
            vmem((n_dp * cap_dp, u_rows), BF16),
            vmem((n_dp, cap_dp, width), BF16),
            vmem((n_dp, cap_dp, width), BF16),
            vmem((n_tab, 2 * cap_t, 128), BF16),
            vmem((n_tab, 2 * cap_t, 128), BF16),
            vmem((n_tab, 1, 128), F32),
            vmem((n_tab, 1, 128), F32),
            vmem((n_dp, w_rows, width), BF16),
            vmem((n_dp, w_rows, width), BF16),
            vmem((n_x, r_rows, width), F32),
            vmem((n_z, r_rows, width), F32),
            vmem((n_z, r_rows, width), F32),
            vmem((n_z, r_rows, width), F32),
            vmem((n_dp, n_z, r_rows, width), F32),
            sem((len(args),)), sem((len(outs),)),
            sem((2, half, 2)), sem((n_dp, 2)), sem((n_y,)), sem((n_y,)),
            sem((n_y,)), sem((n_y,)), sem((2, half, 2)), sem((2, half, 2)),
            sem((8,)), sem((8,)),
        ],
        compiler_params=pltpu.CompilerParams(
            collective_id=0, has_side_effects=True, vmem_limit_bytes=60 << 20
        ),
        name="group_step",
    )(*args)


def place_kernel(got_ref, code_ref, gq_in, gw_in, gg_in, out_ref, gq_ref, gw_ref, gg_ref):
    tile = out_ref.shape[0]
    line = iota((tile, code_ref.shape[1]), 0) + pl.program_id(0) * tile
    hits = (line == code_ref[...]).astype(F32).astype(BF16)
    out_ref[...] = dot(hits, got_ref[...])

    @pl.when(pl.program_id(0) == 0)
    def _():
        gq_ref[...] = gq_in[...]
        gw_ref[...] = gw_in[...]
        gg_ref[...] = gg_in[...]


def place_rows(got, code, *others):
    tile = 512
    n_got, width = got.shape
    whole = lambda a: pl.BlockSpec(a.shape, lambda i: (0, 0))
    return pl.pallas_call(
        place_kernel,
        grid=(ROWS_DEV // tile,),
        out_shape=(jax.ShapeDtypeStruct((ROWS_DEV, width), F32),)
        + tuple(jax.ShapeDtypeStruct(a.shape, a.dtype) for a in others),
        in_specs=[whole(a) for a in (got, code, *others)],
        out_specs=(pl.BlockSpec((tile, width), lambda i: (i, 0)),) + tuple(whole(a) for a in others),
        compiler_params=pltpu.CompilerParams(vmem_limit_bytes=60 << 20),
        name="place_rows",
    )(got, code, *others)


def body(n_dp, n_x, n_z, *args):
    grad_query, got, code, gw, gg = step(n_dp, n_x, n_z, *args)
    grad_table, grad_query, gw, gg = place_rows(got, code, grad_query, gw, gg)
    return grad_query, grad_table, gw, gg.reshape(-1)


def solution(mesh):
    n_x = X_CHIPS
    split = P(("dp", "table"))
    split2 = P(("dp", "table"), None)
    return jax.shard_map(
        functools.partial(body, mesh.shape["dp"], n_x, mesh.shape["table"] // n_x),
        mesh=mesh,
        in_specs=(split2, split2, split, split, split, split, split, P(), P(), P()),
        out_specs=(split2, split2, P(), P()),
        check_vma=False,
    )
```

```python
import functools
import math

import jax
import jax.numpy as jnp
from jax import lax
from jax.experimental import pallas as pl
from jax.experimental.pallas import tpu as pltpu
from jax.sharding import PartitionSpec as P

ROWS_DEV = 2048
NEG = -1e30
INV_TEMP = 20.0
SCALE2 = INV_TEMP * math.log2(math.e)
EXT = 16
CORES = 2
X_CHIPS = 4
MESH = pl.DeviceIdType.MESH
F32 = jnp.float32
BF16 = jnp.bfloat16


def iota(shape, dim):
    return lax.broadcasted_iota(jnp.int32, shape, dim)


def dot(a, b, da=1, db=0):
    return lax.dot_general(a, b, (((da,), (db,)), ((), ())), preferred_element_type=F32)


def split3(x):
    hi = x.astype(BF16).astype(F32)
    mid = (x - hi).astype(BF16).astype(F32)
    low = (x - hi - mid).astype(BF16).astype(F32)
    return hi, mid, low


def step_kernel(
    n_dp, n_x, n_z, cap_dp, cap_t,
    q_hbm, rows_hbm, bin_hbm, cnt_hbm, lab_hbm, own_hbm, loc_hbm, logq_hbm, w_hbm, gain_hbm,
    gq_hbm, got_hbm, code_hbm, gw_hbm, gg_hbm,
    q_ref, rows_ref, bin_ref, cnt_ref, lab_ref, own_ref, loc_ref, logq_ref, w_ref, gain_ref,
    gq_ref, got_ref, code_ref, gw_ref, gg_ref,
    blocks, weights, q_t, z_t, top, total, acc, sib_out, sib_in, ring_out, ring_in,
    mid_meta, base_ref, place, first, mid, second, got, meta_out, meta_in,
    w_out, w_in, x_in, r_out, r_in, row_in, full,
    in_sem, out_sem,
    ag_ring_send, ag_ring_recv, ag_sib_send, ag_sib_recv, rs_sib_send, rs_sib_recv, rs_ring_send, rs_ring_recv,
    all_send, all_recv,
):
    n_tab = n_x * n_z
    n_y = n_dp // CORES
    half = n_y // 2
    u_rows, width = rows_ref.shape
    q_rows = q_ref.shape[0]
    queries_all = q_rows * n_dp * n_tab
    cut = u_rows // 2 + EXT
    subs = (pl.ds(0, cut), pl.ds(cut, u_rows + EXT - cut))
    halves = (pl.ds(0, u_rows // 2), pl.ds(u_rows // 2, u_rows // 2))

    fetches = [
        pltpu.make_async_copy(src, dst, in_sem.at[k])
        for k, (src, dst) in enumerate((
            (rows_hbm, rows_ref), (w_hbm, w_ref), (gain_hbm, gain_ref), (bin_hbm, bin_ref),
            (cnt_hbm, cnt_ref), (own_hbm, own_ref), (loc_hbm, loc_ref), (logq_hbm, logq_ref),
            (q_hbm, q_ref), (lab_hbm, lab_ref),
        ))
    ]
    for fetch in fetches:
        fetch.start()

    me, t = lax.axis_index("dp"), lax.axis_index("table")
    y, c = lax.div(me, CORES), lax.rem(me, CORES)
    x, z = lax.div(t, n_z), lax.rem(t, n_z)
    sib = y * CORES + (1 - c)

    def at(y_pos, core):
        return lax.rem(y_pos + 2 * n_y, n_y) * CORES + core

    up, down = at(y + 1, c), at(y - 1, c)

    def turns(n):
        return [(i + 1) // 2 * (1 if i % 2 else -1) for i in range(n)]

    def dp_each(do):
        for off in turns(n_y):
            y_pos = lax.rem(y + (off + n_y), n_y) * CORES
            if off:
                do(y_pos + c)
            do(y_pos + (1 - c))

    def z_each(do):
        for off in turns(n_z)[1:]:
            do(lax.rem(z + (off + n_z), n_z))

    def x_each(do):
        for off in range(1, n_x):
            do(lax.rem(x + off, n_x))

    def tab_each(do):
        cols = [lax.rem(x + off, n_x) * n_z for off in range(n_x)]
        far = lax.rem(z + n_z // 2, n_z)
        for k, col in enumerate(cols):
            if k:
                do(col + z)
            do(col + far)

        def pair(m, _):
            ahead, behind = lax.rem(z + m, n_z), lax.rem(z + n_z - m, n_z)
            for col in cols:
                do(col + ahead)
                do(col + behind)
            return 0

        lax.fori_loop(1, n_z // 2, pair, 0)

    barrier = pltpu.get_barrier_semaphore()

    def greet(axis):
        return lambda peer: pl.semaphore_signal(
            barrier, inc=1, device_id={axis: peer}, device_id_type=MESH
        )

    dp_each(greet("dp"))
    tab_each(greet("table"))

    for fetch in fetches[:8]:
        fetch.wait()
    rows = rows_ref[...]
    blocks[me, :u_rows, :] = rows
    offs = split3(logq_ref[...] * (-1.0 / INV_TEMP))
    table = jnp.zeros((EXT, logq_ref.shape[1]), F32)
    for k, part in enumerate(offs):
        table = jnp.where(iota(table.shape, 0) == k, part, table)
    hits = (iota((logq_ref.shape[1], u_rows), 0) == bin_ref[...]).astype(F32).astype(BF16)
    ext = dot(table.astype(BF16), hits)
    line = iota(ext.shape, 0)
    dead = iota(ext.shape, 1) >= cnt_ref[...]
    ext = jnp.where(dead, jnp.where(line == 0, NEG, 0.0), ext)
    own, loc = own_ref[...], loc_ref[...]
    bits = n_tab.bit_length() - 1
    fields = (own >> bits, own & (n_tab - 1), loc >> 8, loc & 255)
    for k, part in enumerate(fields):
        ext = jnp.where(line == 3 + k, part.astype(F32), ext)
    blocks[me, u_rows:, :] = ext.astype(BF16)
    for fetch in fetches[8:]:
        fetch.wait()
    q_t[...] = q_ref[...].astype(F32).T.astype(BF16)
    z_t[...] = jnp.zeros_like(z_t)
    ring_in[1, 0, 1] = jnp.zeros((u_rows // 2, width), BF16)
    ring_in[0, 0, 0] = jnp.zeros((u_rows // 2, width), BF16)
    base_ref[...] = jnp.zeros_like(base_ref)

    before = (iota((u_rows, u_rows), 0) < iota((u_rows, u_rows), 1)).astype(F32).astype(BF16)
    own_dp = ext[3:4, :]
    is_dp = (iota((n_dp, u_rows), 0).astype(F32) == own_dp).astype(F32)
    rank = jnp.sum(is_dp * dot(is_dp.astype(BF16), before), axis=0, keepdims=True)
    pos = (own_dp * cap_dp + rank).astype(jnp.int32)
    place[...] = (iota((n_dp * cap_dp, u_rows), 0) == pos).astype(F32).astype(BF16)
    pl.semaphore_wait(barrier, n_dp + n_tab - 2)

    def ring_block(b, sub, d, way):
        return pltpu.make_async_remote_copy(
            src_ref=blocks.at[b, subs[sub]], dst_ref=blocks.at[b, subs[sub]],
            send_sem=ag_ring_send.at[way, d, sub], recv_sem=ag_ring_recv.at[b, sub],
            device_id={"dp": up if way else down}, device_id_type=MESH,
        )

    def to_sib(b):
        return pltpu.make_async_remote_copy(
            src_ref=blocks.at[b], dst_ref=blocks.at[b],
            send_sem=ag_sib_send.at[lax.div(b, CORES)], recv_sem=ag_sib_recv.at[lax.div(b, CORES)],
            device_id={"dp": sib}, device_id_type=MESH,
        )

    pick = (iota((EXT, q_rows), 0) < 3).astype(F32).astype(BF16)

    def score(b):
        rows = blocks[b, :u_rows, :]
        items = (gain_ref[...] * rows.astype(F32) + dot(rows, w_ref[...])).astype(BF16)
        raw = dot(items, q_t[...]) + dot(blocks[b, u_rows:, :], pick, 0, 0)
        high = jnp.max(raw, axis=0, keepdims=True)
        e = jnp.exp2((raw - high) * SCALE2)
        weights[b] = e
        top[b] = high
        total[b] = jnp.sum(e, axis=0, keepdims=True)

    def gather_step(d, _):
        near = (at(y + d, c), at(y - d, c))
        between = (d > 0) & (d < half)
        for sub in (0, 1):
            for way in (1, 0):
                b = near[way]

                @pl.when(between | ((d == half) & (sub == 1 - way)))
                def _():
                    ring_block(b, sub, 0, way).wait_recv()

                forward = d < half if sub == 1 - way else d < half - 1

                @pl.when(forward)
                def _():
                    ring_block(b, sub, d, way).start()

        to_sib(near[1]).start()

        @pl.when(between)
        def _():
            to_sib(near[0]).start()

        def one(j, _):
            score(at(y + (2 * j - 1) * d, c))
            return 0

        lax.fori_loop(0, ways(d), one, 0)

        @pl.when(d > 0)
        def _():
            from_sib(d - 1)

        return 0

    def ways(d):
        return jnp.where((d == 0) | (d == half), 1, 2)

    def from_sib(d):
        def one(j, _):
            b = at(y + (2 * j - 1) * d, 1 - c)
            to_sib(b).wait_recv()
            score(b)
            return 0

        lax.fori_loop(0, ways(d), one, 0)

    lax.fori_loop(0, half + 1, gather_step, 0)
    from_sib(half)

    high = jnp.max(top[...], axis=0)
    rel = jnp.exp2((top[...] - high[None]) * SCALE2)
    mass = jnp.sum(total[...] * rel, axis=0)
    top[...] = rel * (INV_TEMP / mass)[None]

    def sib_copy(slot):
        return pltpu.make_async_remote_copy(
            src_ref=sib_out.at[slot], dst_ref=sib_in.at[slot],
            send_sem=rs_sib_send.at[slot], recv_sem=rs_sib_recv.at[slot],
            device_id={"dp": sib}, device_id_type=MESH,
        )

    def ring_sum(way, k, sub):
        return pltpu.make_async_remote_copy(
            src_ref=ring_out.at[way, k, sub], dst_ref=ring_in.at[way, k, sub],
            send_sem=rs_ring_send.at[way, k, sub], recv_sem=rs_ring_recv.at[way, k, sub],
            device_id={"dp": up if way else down}, device_id_type=MESH,
        )

    def part_of(b):
        lab = jnp.where(b == me, lab_ref[...], -1)
        grad = weights[b] * top[b]
        grad = jnp.where(iota(grad.shape, 0) == lab, grad - INV_TEMP, grad).astype(BF16)
        z_t[...] += dot(blocks[b, :u_rows, :], grad, 0, 0)
        return dot(grad, q_ref[...])

    def event(e, core):
        d, j = half - lax.div(e + 1, 2), lax.rem(e + 1, 2)
        return at(y + (2 * j - 1) * d, core)

    def give_sib(e, _):
        sib_out[e] = part_of(event(e, 1 - c)).astype(BF16)
        sib_copy(e).start()
        return 0

    def take(e):
        part = part_of(event(e, c))
        sib_copy(e).wait_recv()
        return part + sib_in[e].astype(F32)

    DP, TAB, META, W, X, R, ROW, FULL = range(8)

    def send(kind, axis, peer, src, dst):
        pltpu.make_async_remote_copy(
            src_ref=src, dst_ref=dst, send_sem=all_send.at[kind], recv_sem=all_recv.at[kind],
            device_id={axis: peer}, device_id_type=MESH,
        ).start()

    def whole(kind, buf):
        part = buf.at[pl.ds(0, buf.shape[0] - 1)]
        return pltpu.make_async_remote_copy(
            src_ref=part, dst_ref=part, send_sem=all_send.at[kind], recv_sem=all_recv.at[kind],
            device_id={"dp": sib}, device_id_type=MESH,
        )

    me_f = me.astype(F32)
    per = 128 // cap_dp
    n_groups = n_dp // per
    tab_line = iota((n_tab, u_rows), 0).astype(F32)
    spot = iota((128, u_rows), 0).astype(F32)
    ext_line = iota((EXT, u_rows), 0)

    def arrivals(g, _):
        def one(i, carry):
            base, found = carry
            slot = blocks[g * per + i, u_rows:, :].astype(F32)
            here = (slot[3:4, :] == me_f).astype(F32)
            tab, row_hi, row_lo = slot[4:5, :], slot[5:6, :], slot[6:7, :]
            is_tab = jnp.where(tab_line == tab, here, 0.0)
            earlier = dot(is_tab.astype(BF16), before)
            order = jnp.sum(is_tab * (earlier + base), axis=0, keepdims=True)
            nth = jnp.sum(earlier, axis=0, keepdims=True) + float(i * cap_dp)
            base = base + jnp.sum(is_tab, axis=1, keepdims=True)
            meta = jnp.zeros((EXT, u_rows), F32)
            for k, part in enumerate((here, tab, order, row_hi, row_lo)):
                meta = jnp.where(ext_line == k, part * here, meta)
            sel = jnp.where(spot == nth, here, 0.0)
            return base, found + dot(meta.astype(BF16), sel.astype(BF16), 1, 1)

        found = (base_ref[...], jnp.zeros((EXT, 128), F32))
        for i in range(per):
            found = one(i, found)
        base, found = found
        base_ref[...] = base
        mid_meta[:, pl.ds(pl.multiple_of(g * 128, 128), 128)] = found
        return 0

    def ring_step(k):
        for sub in (0, 1):
            for way in (1, 0):
                if k > 1 or sub == 1 - way:
                    ring_sum(way, k - 1, sub).wait_recv()
                so_far = acc[2 * k - 1 + way, halves[sub], :] + ring_in[way, k - 1, sub].astype(F32)
                ring_out[way, k, sub] = so_far.astype(BF16)
                ring_sum(way, k, sub).start()

    def keep(e, _):
        acc[e] = take(e)
        return 0

    give_sib(0, 0)
    far = take(0).astype(BF16)
    for way in (1, 0):
        ring_out[way, 0, 1 - way] = far[halves[1 - way].start : halves[1 - way].start + u_rows // 2]
        ring_sum(way, 0, 1 - way).start()
    lax.fori_loop(1, n_y, give_sib, 0)
    early = 1
    if half > 1:
        early = 3
        lax.fori_loop(1, early, keep, 0)
        ring_step(1)
    lax.fori_loop(early, n_y, keep, 0)

    z_hi = z_t[...].astype(BF16)
    z_low = (z_t[...] - z_hi.astype(F32)).astype(BF16)
    w_out[...] = (dot(z_hi, q_ref[...]) + dot(z_low, q_ref[...])).astype(BF16).reshape(w_out.shape)
    dp_each(lambda p: send(W, "dp", p, w_out.at[p], w_in.at[me]))
    w_in[me] = w_out[me]

    def sum_dp():
        whole(W, w_in).wait_recv()
        r_out[...] = jnp.sum(w_in[...].astype(F32), axis=0).reshape(r_out.shape)
        z_each(lambda p: send(R, "table", x * n_z + p, r_out.at[p], r_in.at[z]))
        r_in[z] = r_out[z]

    def sum_z():
        whole(R, r_in).wait_recv()
        x_in[x] = jnp.sum(r_in[...], axis=0)
        x_each(lambda p: send(X, "table", p * n_z + z, x_in.at[x], x_in.at[x]))

    def some(first_group, last_group):
        lax.fori_loop(first_group, last_group, arrivals, 0)

    work = [
        lambda: (some(0, n_groups // 2), sum_dp()),
        lambda: (some(n_groups // 2, n_groups), sum_z()),
    ]
    for k in range(2, half):
        ring_step(k)
        if work:
            work.pop(0)()
    for do in work:
        do()

    for sub in (0, 1):
        for way in (1, 0):
            if sub == 1 - way or half > 1:
                ring_sum(way, half - 1, sub).wait_recv()
    for sub in (0, 1):
        arrived = ring_in[0, half - 1, sub].astype(F32) + ring_in[1, half - 1, sub].astype(F32)
        acc[n_y - 1, halves[sub], :] += arrived
    ig = acc[n_y - 1]
    row_grad = (gain_ref[...] * ig + dot(ig.astype(BF16), w_ref[...], 1, 1)).astype(BF16)
    first[...] = dot(place[...], row_grad).astype(BF16).reshape(first.shape)
    dp_each(lambda p: send(DP, "dp", p, first.at[p], mid.at[me]))
    mid[me] = first[me]

    whole(X, x_in).wait_recv()
    row_in[z] = jnp.sum(x_in[...], axis=0) * (1.0 / queries_all)
    z_each(lambda p: send(ROW, "table", x * n_z + p, row_in.at[z], row_in.at[z]))

    n_mid = n_dp * cap_dp
    meta = mid_meta[...]
    valid, tab, order, row_hi, row_lo = (meta[k : k + 1, :] for k in range(5))
    tab = jnp.where(valid > 0.5, tab, -1.0)
    is_tab = iota((n_tab, n_mid), 0).astype(F32) == tab
    is_order = (iota((128, n_mid), 0).astype(F32) == order).astype(F32).astype(BF16)

    def spread(value):
        return dot(jnp.where(is_tab, value, 0.0).astype(BF16), is_order, 1, 1)

    code = 256.0 * spread(row_hi) + spread(row_lo) + spread(valid) - 1.0
    meta_out[...] = code.reshape(meta_out.shape)
    tab_each(lambda p: send(META, "table", p, meta_out.at[p], meta_in.at[t]))
    meta_in[t] = meta_out[t]

    pos2 = (tab * cap_t + order).astype(jnp.int32)
    place2 = (iota((n_tab * cap_t, n_mid), 0) == pos2).astype(F32).astype(BF16)

    whole(DP, mid).wait_recv()
    out = dot(place2, mid[...].reshape(n_mid, width)).reshape(n_tab, cap_t, width)
    second[:, :cap_t, :] = out[:, :, :128].astype(BF16)
    second[:, cap_t:, :] = out[:, :, 128:].astype(BF16)
    tab_each(lambda p: send(TAB, "table", p, second.at[p], got.at[t]))
    got[t] = second[t]

    whole(ROW, row_in).wait_recv()
    full[me] = row_in[...]
    dp_each(lambda p: send(FULL, "dp", p, full.at[me], full.at[me]))

    z_all = z_t[...].T
    z_hi = z_all.astype(BF16)
    z_low = (z_all - z_hi.astype(F32)).astype(BF16)
    gq_ref[...] = (gain_ref[...] * z_all + dot(z_hi, w_ref[...]) + dot(z_low, w_ref[...])).astype(BF16)
    gq_copy = pltpu.make_async_copy(gq_ref, gq_hbm, out_sem.at[0])
    gq_copy.start()

    whole(META, meta_in).wait_recv()
    code = meta_in[...].reshape(n_tab, 128).astype(jnp.int32) + 1
    n_got = n_tab * cap_t
    cols = iota((1, n_got), 1)
    is_src = (iota((n_tab, n_got), 0) == lax.div(iota((n_tab, n_got), 1), cap_t)).astype(F32).astype(BF16)

    def along(value):
        return dot(value.astype(F32).astype(BF16), is_src, 0, 0)

    wide = 256.0 * along(code >> 8) + along(code & 255) - 1.0
    mine = iota((128, n_got), 0) == lax.rem(cols, cap_t)
    code_ref[...] = jnp.sum(jnp.where(mine, wide, 0.0), axis=0, keepdims=True).astype(jnp.int32)
    code_copy = pltpu.make_async_copy(code_ref, code_hbm, out_sem.at[1])
    code_copy.start()

    for d in range(half):
        for way in (0, 1):
            for sub in (0, 1):
                if sub == 1 - way or d < half - 1:
                    ring_block(me, sub, d, way).wait_send()
                if sub == 1 - way or d > 0:
                    ring_sum(way, d, sub).wait_send()
    for k in range(n_y):
        to_sib(k * CORES).wait_send()
        sib_copy(k).wait_send()
    for kind, buf in ((W, w_in), (X, x_in), (R, r_in), (ROW, row_in), (META, meta_in), (DP, mid)):
        whole(kind, buf).wait_send()

    whole(FULL, full).wait_recv()
    gw = full[...].reshape(width, width)
    gw_ref[...] = gw
    gw_copy = pltpu.make_async_copy(gw_ref, gw_hbm, out_sem.at[2])
    gw_copy.start()
    diag = iota((width, width), 0) == iota((width, width), 1)
    gg_ref[...] = jnp.sum(jnp.where(diag, gw, 0.0), axis=0, keepdims=True)
    gg_copy = pltpu.make_async_copy(gg_ref, gg_hbm, out_sem.at[3])
    gg_copy.start()

    whole(TAB, got).wait_recv()
    arrived = got[...].astype(F32)
    got_ref[:, :128] = arrived[:, :cap_t, :].reshape(n_got, 128).astype(BF16)
    got_ref[:, 128:] = arrived[:, cap_t:, :].reshape(n_got, 128).astype(BF16)
    got_copy = pltpu.make_async_copy(got_ref, got_hbm, out_sem.at[4])
    got_copy.start()
    whole(TAB, got).wait_send()
    whole(FULL, full).wait_send()
    for copy in (gq_copy, code_copy, gw_copy, gg_copy, got_copy):
        copy.wait()


def step(n_dp, n_x, n_z, queries, item_rows, item_bin, counts, labels, owner, local_row, logq, w, gain):
    q_rows, width = queries.shape
    u_rows = item_rows.shape[0]
    n_tab = n_x * n_z
    n_y = n_dp // CORES
    half = n_y // 2
    cap_dp = max(2, 2 * u_rows // n_dp)
    cap_t = max(2, (n_dp * cap_dp + n_tab - 1) // n_tab)
    w_rows = width // n_dp
    r_rows = w_rows // n_z
    args = (
        queries, item_rows, item_bin[None], counts[None], labels[None], owner[None], local_row[None],
        logq[None], w, gain[None],
    )
    outs = (
        jax.ShapeDtypeStruct((q_rows, width), BF16),
        jax.ShapeDtypeStruct((n_tab * cap_t, width), BF16),
        jax.ShapeDtypeStruct((1, n_tab * cap_t), jnp.int32),
        jax.ShapeDtypeStruct((width, width), F32),
        jax.ShapeDtypeStruct((1, width), F32),
    )
    vmem = pltpu.VMEM
    sem = pltpu.SemaphoreType.DMA
    return pl.pallas_call(
        functools.partial(step_kernel, n_dp, n_x, n_z, cap_dp, cap_t),
        out_shape=outs,
        in_specs=[pl.BlockSpec(memory_space=pl.ANY)] * len(args),
        out_specs=(pl.BlockSpec(memory_space=pl.ANY),) * len(outs),
        scratch_shapes=[vmem(a.shape, a.dtype) for a in args + outs]
        + [
            vmem((n_dp, u_rows + EXT, width), BF16),
            vmem((n_dp, u_rows, q_rows), F32),
            vmem((width, q_rows), BF16),
            vmem((width, q_rows), F32),
            vmem((n_dp, 1, q_rows), F32),
            vmem((n_dp, 1, q_rows), F32),
            vmem((n_y, u_rows, width), F32),
            vmem((n_y, u_rows, width), BF16),
            vmem((n_y, u_rows, width), BF16),
            vmem((2, half, 2, u_rows // 2, width), BF16),
            vmem((2, half, 2, u_rows // 2, width), BF16),
            vmem((EXT, n_dp * cap_dp), F32),
            vmem((n_tab, 1), F32),
            vmem((n_dp * cap_dp, u_rows), BF16),
            vmem((n_dp, cap_dp, width), BF16),
            vmem((n_dp, cap_dp, width), BF16),
            vmem((n_tab, 2 * cap_t, 128), BF16),
            vmem((n_tab, 2 * cap_t, 128), BF16),
            vmem((n_tab, 1, 128), F32),
            vmem((n_tab, 1, 128), F32),
            vmem((n_dp, w_rows, width), BF16),
            vmem((n_dp, w_rows, width), BF16),
            vmem((n_x, r_rows, width), F32),
            vmem((n_z, r_rows, width), F32),
            vmem((n_z, r_rows, width), F32),
            vmem((n_z, r_rows, width), F32),
            vmem((n_dp, n_z, r_rows, width), F32),
            sem((len(args),)), sem((len(outs),)),
            sem((2, half, 2)), sem((n_dp, 2)), sem((n_y,)), sem((n_y,)),
            sem((n_y,)), sem((n_y,)), sem((2, half, 2)), sem((2, half, 2)),
            sem((8,)), sem((8,)),
        ],
        compiler_params=pltpu.CompilerParams(
            collective_id=0, has_side_effects=True, vmem_limit_bytes=60 << 20
        ),
        name="group_step",
    )(*args)


def place_kernel(got_ref, code_ref, gq_in, gw_in, gg_in, out_ref, gq_ref, gw_ref, gg_ref):
    tile = out_ref.shape[0]
    line = iota((tile, code_ref.shape[1]), 0) + pl.program_id(0) * tile
    hits = (line == code_ref[...]).astype(F32).astype(BF16)
    out_ref[...] = dot(hits, got_ref[...])

    @pl.when(pl.program_id(0) == 0)
    def _():
        gq_ref[...] = gq_in[...]
        gw_ref[...] = gw_in[...]
        gg_ref[...] = gg_in[...]


def place_rows(got, code, *others):
    tile = 512
    n_got, width = got.shape
    whole = lambda a: pl.BlockSpec(a.shape, lambda i: (0, 0))
    return pl.pallas_call(
        place_kernel,
        grid=(ROWS_DEV // tile,),
        out_shape=(jax.ShapeDtypeStruct((ROWS_DEV, width), F32),)
        + tuple(jax.ShapeDtypeStruct(a.shape, a.dtype) for a in others),
        in_specs=[whole(a) for a in (got, code, *others)],
        out_specs=(pl.BlockSpec((tile, width), lambda i: (i, 0)),) + tuple(whole(a) for a in others),
        compiler_params=pltpu.CompilerParams(vmem_limit_bytes=60 << 20),
        name="place_rows",
    )(got, code, *others)


def body(n_dp, n_x, n_z, *args):
    grad_query, got, code, gw, gg = step(n_dp, n_x, n_z, *args)
    grad_table, grad_query, gw, gg = place_rows(got, code, grad_query, gw, gg)
    return grad_query, grad_table, gw, gg.reshape(-1)


def solution(mesh):
    n_x = X_CHIPS
    split = P(("dp", "table"))
    split2 = P(("dp", "table"), None)
    return jax.shard_map(
        functools.partial(body, mesh.shape["dp"], n_x, mesh.shape["table"] // n_x),
        mesh=mesh,
        in_specs=(split2, split2, split, split, split, split, split, P(), P(), P()),
        out_specs=(split2, split2, P(), P()),
        check_vma=False,
    )
```
